32 devices in a mesh: scen: 2 (over x), trade: 16 (over z, y, core).
Axes of the slice: x: 2, y: 2, z: 4, core: 2. Of those that a mesh axis runs over, the one named last changes fastest.
Arguments:
- coefficients: bfloat16 [32768, 256], P('trade'), may hold values from -0.375 to 0.375
- scenario_basis: bfloat16 [256, 16, 256], P('trade', None, 'scen'), parts along dimension 2, may hold values from -6 to 6
- trade_set: int32 [32768], P('trade'), may hold values from 0 to 1023, as said below
- option_flag: int32 [32768], P('trade'), may hold values 0 or 1
- margin_lag: int32 [1024], P('trade'), may hold values from 1 to 3
Outputs:
- exposure: float32 [1024, 16, 256], P('trade', None, 'scen'), parts along dimension 2
The draws below stay inside these ranges and needn't reach their ends.
There are 2 independent parts, one for each index of `scen`. The reference program is written for one: setup_inputs(seed, part) draws one part's arguments, and reference() takes and returns one part's arrays. A program takes and returns all parts, laid end to end along the dimension named above; an argument that names none is the same for every part. Nothing has to cross between parts.
Inputs may be any that keep to these rules, and one draw needn't show every extreme that they name: `trade_set`: set j belongs to owner j // 64. The trades of one device (aligned blocks of 2048 trades) name at most 8 distinct sets of any one owner; in every draw each device names exactly 8 sets of some owner, and some owner has 8 of its sets named by every device.
All inputs are finite; a program needn't handle non-finite values. No bound on the sum of `option_flag` on one device may be relied on, other than what follows from the above.
Results may differ from the reference program's by a relative error of at most 0.0027.
Values may be sent and summed in bfloat16 or wider, within the bound.
A program may use at most 128 MiB of HBM per device.

```python
import jax
import jax.numpy as jnp
from jax import lax

F = 256
S = 128
DT = 16
TR_DEV = 2048
SETS_DEV = 64
CAP = 8
LAG_MAX = 3
TRADES = 32768
NS = 1024
N_TRADE = 16


def draw_trade_set(key, part):
    key = jax.random.fold_in(key, 11)
    owners = NS // SETS_DEV
    slot_count = owners * CAP
    shared_owner = jax.random.randint(jax.random.fold_in(key, 1), (), 0, owners)
    slot_owner = jnp.repeat(jnp.arange(owners), CAP)
    slot_rank = jnp.tile(jnp.arange(CAP), owners)

    def one_device(device_key):
        subkeys = jax.random.split(device_key, 6)
        per_owner = jax.random.randint(subkeys[0], (owners,), 1, CAP + 1)
        single = jax.random.randint(subkeys[1], (), 0, owners)
        forced = (jnp.arange(owners) == single) | (jnp.arange(owners) == shared_owner)
        per_owner = jnp.where(forced, CAP, per_owner)
        chosen = jax.vmap(lambda subkey: jax.random.permutation(subkey, SETS_DEV)[:CAP])(jax.random.split(subkeys[2], owners))
        valid = slot_rank < per_owner[slot_owner]
        scores = jax.random.randint(subkeys[3], (slot_count,), 0, slot_count)
        scores = jnp.where(valid, scores, slot_count) * slot_count + jnp.arange(slot_count)
        ranking = jnp.argsort(scores)
        live_count = jnp.sum(valid.astype(jnp.int32))
        further = jax.random.randint(subkeys[4], (TR_DEV,), 0, live_count)
        positions = jnp.arange(TR_DEV)
        chosen_slot = ranking[jnp.where(positions < live_count, jnp.minimum(positions, slot_count - 1), further)]
        set_ids = slot_owner[chosen_slot] * SETS_DEV + chosen.reshape(-1)[chosen_slot]
        return set_ids[jax.random.permutation(subkeys[5], TR_DEV)]
    device_keys = jax.random.split(key, owners)
    return jax.vmap(one_device)(device_keys).reshape(-1).astype(jnp.int32)


def with_ends(array, key, least, high):
    index_at = [jax.random.randint(jax.random.fold_in(key, axis), (), 0, length) for axis, length in enumerate(array.shape)]
    main_axis = array.shape.index(max(array.shape))
    beside = index_at[:main_axis] + [(index_at[main_axis] + 1) % array.shape[main_axis]] + index_at[main_axis + 1:]
    return array.at[tuple(index_at)].set(least).at[tuple(beside)].set(high)


def steps_of(own_key, shape, cuts, low, high):
    level = 1.0
    for position, shards_of in cuts:
        draws = jax.random.uniform(jax.random.fold_in(jax.random.fold_in(own_key, 6), position), (shards_of,), jnp.float32, low / len(cuts), high / len(cuts))
        level = level * jnp.repeat(jnp.exp(draws), shape[position] // shards_of).reshape((-1,) + (1,) * (len(shape) - 1 - position))
    return level


def scatter_about(key, extent, scale, limit, cuts=(), kind=jnp.bfloat16):
    values = jax.random.normal(key, extent, jnp.float32) * scale
    if len(cuts) > 0:
        values = steps_of(key, extent, cuts, -0.22, 0.18) * values
    return jnp.clip(values, min=-limit, max=limit).astype(kind)


def setup_inputs(seed: int = 0, part: int = 0) -> dict:
    key_list = jax.random.split(jax.random.key(seed), 6)
    own_keys = jax.random.split(jax.random.fold_in(key_list[5], part), 6)
    coefficients = scatter_about(key_list[0], (TRADES, F), F ** -0.5, 0.375, ((0, 16),))
    scenario_basis = scatter_about(own_keys[1], (F, DT, S), 1.0, 6.0, ((0, 16),))
    trade_set = draw_trade_set(jax.random.fold_in(key_list[5], 71), part)
    option_flag = with_ends((jax.random.randint(key_list[3], (TRADES,), 0, 2) < 1).astype(jnp.int32), jax.random.fold_in(key_list[3], 1), 0, 1)
    margin_lag = with_ends(jax.random.randint(key_list[4], (NS,), 1, LAG_MAX + 1), jax.random.fold_in(key_list[4], 1), 1, LAG_MAX).astype(jnp.int32)
    return dict(coefficients=coefficients, scenario_basis=scenario_basis, trade_set=trade_set, option_flag=option_flag, margin_lag=margin_lag)


def collateralise(netted, margin_lag):
    collateral = jnp.zeros_like(netted)
    for offset in range(1, LAG_MAX + 1):
        shifted = jnp.concatenate([jnp.zeros_like(netted[:, :offset]), netted[:, :-offset]], axis=1)
        collateral = jnp.where((margin_lag == offset)[:, None, None], shifted, collateral)
    return jnp.maximum(netted - collateral, 0.0)


def reference(coefficients, scenario_basis, trade_set, option_flag, margin_lag):
    basis_flat = scenario_basis.reshape(F, DT * S)
    coef_blocks = coefficients.reshape(N_TRADE, TR_DEV, F)
    set_blocks = trade_set.reshape(N_TRADE, TR_DEV)
    flag_blocks = option_flag.reshape(N_TRADE, TR_DEV)

    def tally(cumulative_credit_risk, inputs):
        fitted_weight_matrix, counterparty_group_list, callable_marker_list = inputs
        appraised_contracts = jnp.dot(fitted_weight_matrix, basis_flat, preferred_element_type=jnp.float32)
        estimated_worth = jnp.where(callable_marker_list[:, None] == 1, jnp.maximum(appraised_contracts, 0.0), appraised_contracts).astype(jnp.bfloat16)
        return cumulative_credit_risk.at[counterparty_group_list].add(estimated_worth.astype(jnp.float32)), None

    netted, _ = lax.scan(tally, jnp.zeros((NS, DT * S), jnp.float32), (coef_blocks, set_blocks, flag_blocks))
    return collateralise(netted.reshape(NS, DT, S), margin_lag)
```

```python
import functools

import jax
import jax.numpy as jnp
from jax import lax
from jax.experimental import pallas as pl
from jax.experimental.pallas import tpu as pltpu
from jax.sharding import PartitionSpec as P

SETS_DEV = 64
CAP = 8
LAG_MAX = 3
LANES = 128
INNER = 4
DATES_STEP = 4
ROWS_STEP = 512


def kernel(n, gathers, dates, coef_ref, basis_ref, set_ref, flag_ref, lag_ref, out_ref,
           whole, floor, member, sums, send, recv, ids_out, ids_in, lags_in, pick,
           bs_sem, br_sem, is_sem, ir_sem, ls_sem, lr_sem, ps_sem, pr_sem, *more):
    me = lax.axis_index("trade")
    slots = n * CAP
    trades = coef_ref.shape[0]
    steps = dates // DATES_STEP
    width = DATES_STEP * LANES

    def remote(src, dst, s_sem, r_sem, to):
        return pltpu.make_async_remote_copy(
            src_ref=src, dst_ref=dst, send_sem=s_sem, recv_sem=r_sem,
            device_id={"trade": to}, device_id_type=pl.DeviceIdType.MESH)

    def others(act):
        def go(k, carry):
            act(lax.rem(me + k, n))
            return carry
        lax.fori_loop(1, n, go, 0)

    barrier = pltpu.get_barrier_semaphore()
    others(lambda to: pl.semaphore_signal(
        barrier, inc=1, device_id={"trade": to}, device_id_type=pl.DeviceIdType.MESH))
    pl.semaphore_wait(barrier, n - 1)

    outer = n // INNER
    place, inner = me // INNER, lax.rem(me, INNER)
    core = lax.rem(inner, 2)
    sibling = place * INNER + inner - core + (1 - core)
    across = place * INNER + lax.rem(inner + 2, INNER)

    def block(owner, to, via):
        src = basis_ref if owner is me else whole.at[owner]
        return remote(src, whole.at[owner], bs_sem.at[via, owner], br_sem.at[owner], to)

    columns = [lax.rem(place + k, outer) for k in range(outer)]
    if gathers:
        for k in range(1, outer):
            block(me, columns[k] * INNER + inner, k - 1).start()
        block(me, across, outer - 1).start()
        block(me, sibling, outer).start()

    others(lambda to: remote(lag_ref, lags_in.at[me], ls_sem.at[to], lr_sem.at[me], to).start())
    lags_in[me] = lag_ref[...]
    if gathers:
        whole[me] = basis_ref[...]

    trade_set = set_ref[...]
    owner_row = trade_set // SETS_DEV
    local_row = trade_set - owner_row * SETS_DEV
    slot_of = lax.broadcasted_iota(jnp.int32, (slots, 1), 0)
    local_of = lax.broadcasted_iota(jnp.int32, (LANES, 1), 0)
    by_owner = (owner_row == slot_of // CAP).astype(jnp.float32).astype(jnp.bfloat16)
    by_local = (local_row == local_of).astype(jnp.float32).astype(jnp.bfloat16)
    counts = lax.dot_general(by_owner, by_local, (((1,), (1,)), ((), ())),
                             preferred_element_type=jnp.float32)
    present = counts > 0.5
    before = (lax.broadcasted_iota(jnp.int32, (LANES, LANES), 0)
              < lax.broadcasted_iota(jnp.int32, (LANES, LANES), 1))
    rank = jnp.dot(present.astype(jnp.float32).astype(jnp.bfloat16),
                   before.astype(jnp.float32).astype(jnp.bfloat16),
                   preferred_element_type=jnp.float32)
    chosen = present & (rank == lax.rem(slot_of, CAP).astype(jnp.float32))
    lane = lax.broadcasted_iota(jnp.int32, (slots, LANES), 1)
    local = jnp.sum(jnp.where(chosen, lane + 1, 0).astype(jnp.float32), axis=1, keepdims=True) - 1.0
    ids_out[...] = jnp.broadcast_to(local, (slots, LANES)).reshape(n, CAP, LANES)
    ids_in[me] = ids_out[me]
    others(lambda to: remote(
        ids_out.at[to], ids_in.at[me], is_sem.at[to], ir_sem.at[me], to).start())
    name = jnp.where(local < 0.0, -1, local.astype(jnp.int32) + (slot_of // CAP) * SETS_DEV)
    member[...] = (name == trade_set).astype(jnp.float32).astype(jnp.bfloat16)

    if gathers:
        for k in range(1, outer):
            owner = columns[k] * INNER + inner
            block(owner, owner, 0).wait_recv()
            block(owner, across, outer - 1).start()
            block(owner, sibling, outer).start()

    lowest = jnp.where(flag_ref[...] == 1, 0.0, -3.0e38).astype(jnp.float32)
    floor[...] = jnp.broadcast_to(lowest, (LANES, trades)).T

    others(lambda src: remote(
        lag_ref, lags_in.at[src], ls_sem.at[src], lr_sem.at[src], src).wait_recv())
    lag = jnp.sum(jnp.where(chosen, lags_in[...].reshape(slots, LANES), 0.0), axis=1, keepdims=True)
    lag = jnp.broadcast_to(lag, (slots, LANES))
    sums[0:LAG_MAX] = jnp.zeros((LAG_MAX, slots, LANES), jnp.float32)

    if gathers:
        for k in range(outer):
            owner = columns[k] * INNER + lax.rem(inner + 2, INNER)
            block(owner, owner, 0).wait_recv()
            block(owner, sibling, outer).start()

    others(lambda src: remote(
        ids_out.at[src], ids_in.at[src], is_sem.at[src], ir_sem.at[src], src).wait_recv())
    ids = ids_in[...]
    ids = jnp.concatenate([ids, ids], axis=1).reshape(n * 2 * CAP, LANES)
    row = lax.broadcasted_iota(jnp.int32, (n * 2 * CAP, LANES), 0)
    lane = lax.broadcasted_iota(jnp.int32, (n * 2 * CAP, LANES), 1)
    same = (lax.rem(row, 2 * CAP) // CAP) == lane // SETS_DEV
    hit = same & (ids == lax.rem(lane, SETS_DEV).astype(jnp.float32))
    pick[...] = jnp.where(hit, 1.0, 0.0).astype(jnp.float32).T.astype(jnp.bfloat16)

    if gathers:
        for pair in range(INNER // 2):
            for k in range(outer):
                owner = columns[k] * INNER + lax.rem(inner - core + (1 - core) + 2 * pair, INNER)
                block(owner, owner, 0).wait_recv()

    def basis_at(c):
        cols = pl.ds(pl.multiple_of(c * width, width), width)
        if gathers:
            return whole[:, :, cols].reshape(-1, width)
        return basis_ref[:, cols]

    def piece(c, to):
        return remote(send.at[c, to], recv.at[c, me], ps_sem.at[c, to], pr_sem.at[c, me], to)

    def step(c, carry):
        basis = basis_at(c)
        total = jnp.zeros((slots, width), jnp.float32)
        for first in range(0, trades, ROWS_STEP):
            rows = pl.ds(first, ROWS_STEP)
            valued = jnp.dot(coef_ref[rows, :], basis, preferred_element_type=jnp.float32)
            valued = jnp.maximum(valued, jnp.concatenate([floor[rows, :]] * DATES_STEP, axis=1))
            total += jnp.dot(member[:, rows], valued.astype(jnp.bfloat16),
                             preferred_element_type=jnp.float32)
        for d in range(DATES_STEP):
            sums[LAG_MAX + d] = total[:, d * LANES:(d + 1) * LANES]
        for half in range(DATES_STEP // 2):
            both = []
            for parity in range(2):
                at = LAG_MAX + 2 * half + parity
                collateral = jnp.zeros((slots, LANES), jnp.float32)
                for offset in range(1, LAG_MAX + 1):
                    collateral = jnp.where(lag == float(offset), sums[at - offset], collateral)
                both.append((sums[at] - collateral).reshape(n, CAP, LANES))
            send[c, :, half] = jnp.concatenate(both, axis=1).astype(jnp.bfloat16)
        for k in range(LAG_MAX):
            sums[k] = sums[DATES_STEP + k]
        recv[c, me] = send[c, me]
        others(lambda to: piece(c, to).start())
        return carry

    lax.fori_loop(0, steps, step, 0)

    def finish(c, carry):
        others(lambda src: remote(
            send.at[c, src], recv.at[c, src], ps_sem.at[c, src], pr_sem.at[c, src], src).wait_recv())
        for half in range(DATES_STEP // 2):
            result = jnp.dot(pick[...], recv[c, :, half].reshape(n * 2 * CAP, LANES),
                             preferred_element_type=jnp.float32)
            result = jnp.maximum(result, 0.0)
            for parity in range(2):
                at = pl.multiple_of((c * DATES_STEP + 2 * half + parity) * LANES, LANES)
                out_ref[:, pl.ds(at, LANES)] = result[parity * SETS_DEV:(parity + 1) * SETS_DEV]
        return carry

    lax.fori_loop(0, steps, finish, 0)

    if gathers:
        for k in range(1, outer):
            block(me, me, k - 1).wait_send()
        for k in range(outer):
            owner = columns[k] * INNER + inner
            block(owner, across, outer - 1).wait_send()
            block(owner, sibling, outer).wait_send()
            owner = columns[k] * INNER + lax.rem(inner + 2, INNER)
            block(owner, sibling, outer).wait_send()

    def sent(to):
        remote(lag_ref, lags_in.at[me], ls_sem.at[to], lr_sem.at[me], to).wait_send()
        remote(ids_out.at[to], ids_in.at[me], is_sem.at[to], ir_sem.at[me], to).wait_send()
        for c in range(steps):
            piece(c, to).wait_send()

    others(sent)


def body(coefficients, scenario_basis, trade_set, option_flag, margin_lag):
    n = lax.axis_size("trade")
    share, dates, scenarios = scenario_basis.shape
    trades, features = coefficients.shape
    columns = dates * scenarios
    gathers = share % 16 == 0 and n % INNER == 0
    basis = scenario_basis.reshape(share, columns)
    if not gathers:
        basis = lax.all_gather(basis, "trade", axis=0, tiled=True)
    lags = jnp.pad(margin_lag.astype(jnp.float32), (0, LANES - SETS_DEV))
    lags = jnp.broadcast_to(lags[None, :], (CAP, LANES))
    slots = n * CAP
    steps = dates // DATES_STEP
    halves = DATES_STEP // 2
    dma = pltpu.SemaphoreType.DMA
    whole = (n, share, columns) if gathers else (1, 16, LANES)
    out = pl.pallas_call(
        functools.partial(kernel, n, gathers, dates),
        out_shape=jax.ShapeDtypeStruct((SETS_DEV, columns), jnp.float32),
        in_specs=[pl.BlockSpec(memory_space=pltpu.VMEM)] * 5,
        out_specs=pl.BlockSpec(memory_space=pltpu.VMEM),
        scratch_shapes=[
            pltpu.VMEM(whole, jnp.bfloat16),
            pltpu.VMEM((trades, LANES), jnp.float32),
            pltpu.VMEM((slots, trades), jnp.bfloat16),
            pltpu.VMEM((LAG_MAX + DATES_STEP, slots, LANES), jnp.float32),
            pltpu.VMEM((steps, n, halves, 2 * CAP, LANES), jnp.bfloat16),
            pltpu.VMEM((steps, n, halves, 2 * CAP, LANES), jnp.bfloat16),
            pltpu.VMEM((n, CAP, LANES), jnp.float32),
            pltpu.VMEM((n, CAP, LANES), jnp.float32),
            pltpu.VMEM((n, CAP, LANES), jnp.float32),
            pltpu.VMEM((LANES, n * 2 * CAP), jnp.bfloat16),
            dma((n // INNER + 1, n)),
            dma((n,)),
            dma((n,)),
            dma((n,)),
            dma((n,)),
            dma((n,)),
            dma((steps, n)),
            dma((steps, n)),
        ],
        compiler_params=pltpu.CompilerParams(
            collective_id=0, has_side_effects=True, vmem_limit_bytes=48 * 1024 * 1024
        ),
        cost_estimate=pl.CostEstimate(
            flops=2 * trades * columns * (features + slots),
            bytes_accessed=4 * 1024 * 1024, transcendentals=0,
        ),
    )(coefficients, basis, trade_set[None, :], option_flag[None, :], lags)
    return out.reshape(SETS_DEV, dates, scenarios)


def solution(mesh):
    placed = (P("trade", None), P("trade", None, "scen"), P("trade"), P("trade"), P("trade"))
    return jax.shard_map(
        body, mesh=mesh, in_specs=placed, out_specs=P("trade", None, "scen"), check_vma=False
    )
```

```python
import functools

import jax
import jax.numpy as jnp
from jax import lax
from jax.experimental import pallas as pl
from jax.experimental.pallas import tpu as pltpu
from jax.sharding import PartitionSpec as P

SETS_DEV = 64
CAP = 8
LAG_MAX = 3
LANES = 128
INNER = 4
DATES_STEP = 4
ROWS_STEP = 2048
CUTS = 2


def kernel(n, gathers, dates, coef_hbm, basis_ref, set_ref, flag_ref, lag_ref, out_ref,
           coef_ref, coef_sem, whole, floor, member, sums, send, recv, ids_out, ids_in, lags_in, pick,
           bs_sem, br_sem, is_sem, ir_sem, ls_sem, lr_sem, ps_sem, pr_sem):
    me = lax.axis_index("trade")
    slots = n * CAP
    trades = coef_ref.shape[0]
    steps = dates // DATES_STEP
    width = DATES_STEP * LANES

    load = pltpu.make_async_copy(coef_hbm, coef_ref, coef_sem)
    load.start()

    def remote(src, dst, s_sem, r_sem, to):
        return pltpu.make_async_remote_copy(
            src_ref=src, dst_ref=dst, send_sem=s_sem, recv_sem=r_sem,
            device_id={"trade": to}, device_id_type=pl.DeviceIdType.MESH)

    def others(act):
        def go(k, carry):
            act(lax.rem(me + k, n))
            return carry
        lax.fori_loop(1, n, go, 0)

    barrier = pltpu.get_barrier_semaphore()
    others(lambda to: pl.semaphore_signal(
        barrier, inc=1, device_id={"trade": to}, device_id_type=pl.DeviceIdType.MESH))
    pl.semaphore_wait(barrier, n - 1)

    outer = n // INNER
    place, inner = me // INNER, lax.rem(me, INNER)
    core = lax.rem(inner, 2)
    sibling = place * INNER + inner - core + (1 - core)
    across = place * INNER + lax.rem(inner + 2, INNER)

    cut = dates * LANES // CUTS

    def block(part, owner, to, via):
        cols = pl.ds(part * cut, cut)
        src = basis_ref.at[:, cols] if owner is me else whole.at[owner, :, cols]
        return remote(src, whole.at[owner, :, cols], bs_sem.at[part, via, owner],
                      br_sem.at[part, owner], to)

    def pass_columns(part):
        for k in range(1, outer):
            owner = columns[k] * INNER + inner
            block(part, owner, owner, 0).wait_recv()
            block(part, owner, across, outer - 1).start()
            block(part, owner, sibling, outer).start()

    def pass_across(part):
        for k in range(outer):
            owner = columns[k] * INNER + lax.rem(inner + 2, INNER)
            block(part, owner, owner, 0).wait_recv()
            block(part, owner, sibling, outer).start()

    def end_gather(part):
        for pair in range(INNER // 2):
            for k in range(outer):
                owner = columns[k] * INNER + lax.rem(inner - core + (1 - core) + 2 * pair, INNER)
                block(part, owner, owner, 0).wait_recv()

    columns = [lax.rem(place + k, outer) for k in range(outer)]
    if gathers:
        for part in range(CUTS):
            for k in range(1, outer):
                block(part, me, columns[k] * INNER + inner, k - 1).start()
            block(part, me, across, outer - 1).start()
            block(part, me, sibling, outer).start()

    others(lambda to: remote(lag_ref, lags_in.at[me], ls_sem.at[to], lr_sem.at[me], to).start())
    lags_in[me] = lag_ref[...]
    if gathers:
        whole[me] = basis_ref[...]

    trade_set = set_ref[...]
    owner_row = trade_set // SETS_DEV
    local_row = trade_set - owner_row * SETS_DEV
    slot_of = lax.broadcasted_iota(jnp.int32, (slots, 1), 0)
    local_of = lax.broadcasted_iota(jnp.int32, (LANES, 1), 0)
    by_owner = (owner_row == slot_of // CAP).astype(jnp.float32).astype(jnp.bfloat16)
    by_local = (local_row == local_of).astype(jnp.float32).astype(jnp.bfloat16)
    counts = lax.dot_general(by_owner, by_local, (((1,), (1,)), ((), ())),
                             preferred_element_type=jnp.float32)
    present = counts > 0.5
    before = (lax.broadcasted_iota(jnp.int32, (LANES, LANES), 0)
              < lax.broadcasted_iota(jnp.int32, (LANES, LANES), 1))
    rank = jnp.dot(present.astype(jnp.float32).astype(jnp.bfloat16),
                   before.astype(jnp.float32).astype(jnp.bfloat16),
                   preferred_element_type=jnp.float32)
    chosen = present & (rank == lax.rem(slot_of, CAP).astype(jnp.float32))
    lane = lax.broadcasted_iota(jnp.int32, (slots, LANES), 1)
    local = jnp.sum(jnp.where(chosen, lane + 1, 0).astype(jnp.float32), axis=1, keepdims=True) - 1.0
    ids_out[...] = jnp.broadcast_to(local, (slots, LANES)).reshape(n, CAP, LANES)
    ids_in[me] = ids_out[me]
    others(lambda to: remote(
        ids_out.at[to], ids_in.at[me], is_sem.at[to], ir_sem.at[me], to).start())
    name = jnp.where(local < 0.0, -1, local.astype(jnp.int32) + (slot_of // CAP) * SETS_DEV)
    member[...] = (name == trade_set).astype(jnp.float32).astype(jnp.bfloat16)

    if gathers:
        pass_columns(0)

    lowest = jnp.where(flag_ref[...] == 1, 0.0, -3.0e38).astype(jnp.float32)
    floor[...] = jnp.broadcast_to(lowest, (LANES, trades)).T

    others(lambda src: remote(
        lag_ref, lags_in.at[src], ls_sem.at[src], lr_sem.at[src], src).wait_recv())
    lag = jnp.sum(jnp.where(chosen, lags_in[...].reshape(slots, LANES), 0.0), axis=1, keepdims=True)
    lag = jnp.broadcast_to(lag, (slots, LANES))
    sums[0:LAG_MAX] = jnp.zeros((LAG_MAX, slots, LANES), jnp.float32)

    if gathers:
        pass_across(0)
        for part in range(1, CUTS):
            pass_columns(part)

    others(lambda src: remote(
        ids_out.at[src], ids_in.at[src], is_sem.at[src], ir_sem.at[src], src).wait_recv())
    ids = ids_in[...]
    ids = jnp.concatenate([ids, ids], axis=1).reshape(n * 2 * CAP, LANES)
    row = lax.broadcasted_iota(jnp.int32, (n * 2 * CAP, LANES), 0)
    lane = lax.broadcasted_iota(jnp.int32, (n * 2 * CAP, LANES), 1)
    same = (lax.rem(row, 2 * CAP) // CAP) == lane // SETS_DEV
    hit = same & (ids == lax.rem(lane, SETS_DEV).astype(jnp.float32))
    pick[...] = jnp.where(hit, 1.0, 0.0).astype(jnp.float32).T.astype(jnp.bfloat16)

    load.wait()
    if gathers:
        end_gather(0)

    def basis_at(c):
        cols = pl.ds(pl.multiple_of(c * width, width), width)
        if gathers:
            return whole[:, :, cols].reshape(-1, width)
        return basis_ref[:, cols]

    def piece(c, to):
        return remote(send.at[c, to], recv.at[c, me], ps_sem.at[c, to], pr_sem.at[c, me], to)

    def step(c, carry):
        basis = basis_at(c)
        total = jnp.zeros((slots, width), jnp.float32)
        for first in range(0, trades, ROWS_STEP):
            rows = pl.ds(first, ROWS_STEP)
            valued = jnp.dot(coef_ref[rows, :], basis, preferred_element_type=jnp.float32)
            valued = jnp.maximum(valued, jnp.concatenate([floor[rows, :]] * DATES_STEP, axis=1))
            total += jnp.dot(member[:, rows], valued.astype(jnp.bfloat16),
                             preferred_element_type=jnp.float32)
        for d in range(DATES_STEP):
            sums[LAG_MAX + d] = total[:, d * LANES:(d + 1) * LANES]
        for half in range(DATES_STEP // 2):
            both = []
            for parity in range(2):
                at = LAG_MAX + 2 * half + parity
                collateral = jnp.zeros((slots, LANES), jnp.float32)
                for offset in range(1, LAG_MAX + 1):
                    collateral = jnp.where(lag == float(offset), sums[at - offset], collateral)
                both.append((sums[at] - collateral).reshape(n, CAP, LANES))
            send[c, :, half] = jnp.concatenate(both, axis=1).astype(jnp.bfloat16)
        for k in range(LAG_MAX):
            sums[k] = sums[DATES_STEP + k]
        recv[c, me] = send[c, me]
        others(lambda to: piece(c, to).start())
        return carry

    per_cut = steps // CUTS
    for part in range(CUTS):
        if gathers and part > 0:
            end_gather(part)
        lax.fori_loop(part * per_cut, part * per_cut + 1, step, 0)
        if gathers and part + 1 < CUTS:
            pass_across(part + 1)
        lax.fori_loop(part * per_cut + 1, (part + 1) * per_cut, step, 0)

    def finish(c, carry):
        others(lambda src: remote(
            send.at[c, src], recv.at[c, src], ps_sem.at[c, src], pr_sem.at[c, src], src).wait_recv())
        for half in range(DATES_STEP // 2):
            result = jnp.dot(pick[...], recv[c, :, half].reshape(n * 2 * CAP, LANES),
                             preferred_element_type=jnp.float32)
            result = jnp.maximum(result, 0.0)
            for parity in range(2):
                at = pl.multiple_of((c * DATES_STEP + 2 * half + parity) * LANES, LANES)
                out_ref[:, pl.ds(at, LANES)] = result[parity * SETS_DEV:(parity + 1) * SETS_DEV]
        return carry

    lax.fori_loop(0, steps, finish, 0)

    if gathers:
        for part in range(CUTS):
            for k in range(1, outer):
                block(part, me, me, k - 1).wait_send()
            for k in range(outer):
                owner = columns[k] * INNER + inner
                block(part, owner, across, outer - 1).wait_send()
                block(part, owner, sibling, outer).wait_send()
                owner = columns[k] * INNER + lax.rem(inner + 2, INNER)
                block(part, owner, sibling, outer).wait_send()

    def sent(to):
        remote(lag_ref, lags_in.at[me], ls_sem.at[to], lr_sem.at[me], to).wait_send()
        remote(ids_out.at[to], ids_in.at[me], is_sem.at[to], ir_sem.at[me], to).wait_send()
        for c in range(steps):
            piece(c, to).wait_send()

    others(sent)


def body(coefficients, scenario_basis, trade_set, option_flag, margin_lag):
    n = lax.axis_size("trade")
    share, dates, scenarios = scenario_basis.shape
    trades, features = coefficients.shape
    columns = dates * scenarios
    gathers = share % 16 == 0 and n % INNER == 0
    basis = scenario_basis.reshape(share, columns)
    if not gathers:
        basis = lax.all_gather(basis, "trade", axis=0, tiled=True)
    lags = jnp.pad(margin_lag.astype(jnp.float32), (0, LANES - SETS_DEV))
    lags = jnp.broadcast_to(lags[None, :], (CAP, LANES))
    slots = n * CAP
    steps = dates // DATES_STEP
    halves = DATES_STEP // 2
    dma = pltpu.SemaphoreType.DMA
    whole = (n, share, columns) if gathers else (1, 16, LANES)
    out = pl.pallas_call(
        functools.partial(kernel, n, gathers, dates),
        out_shape=jax.ShapeDtypeStruct((SETS_DEV, columns), jnp.float32),
        in_specs=[pl.BlockSpec(memory_space=pl.ANY)] + [pl.BlockSpec(memory_space=pltpu.VMEM)] * 4,
        out_specs=pl.BlockSpec(memory_space=pltpu.VMEM),
        scratch_shapes=[
            pltpu.VMEM((trades, features), jnp.bfloat16),
            dma(()),
            pltpu.VMEM(whole, jnp.bfloat16),
            pltpu.VMEM((trades, LANES), jnp.float32),
            pltpu.VMEM((slots, trades), jnp.bfloat16),
            pltpu.VMEM((LAG_MAX + DATES_STEP, slots, LANES), jnp.float32),
            pltpu.VMEM((steps, n, halves, 2 * CAP, LANES), jnp.bfloat16),
            pltpu.VMEM((steps, n, halves, 2 * CAP, LANES), jnp.bfloat16),
            pltpu.VMEM((n, CAP, LANES), jnp.float32),
            pltpu.VMEM((n, CAP, LANES), jnp.float32),
            pltpu.VMEM((n, CAP, LANES), jnp.float32),
            pltpu.VMEM((LANES, n * 2 * CAP), jnp.bfloat16),
            dma((CUTS, n // INNER + 1, n)),
            dma((CUTS, n)),
            dma((n,)),
            dma((n,)),
            dma((n,)),
            dma((n,)),
            dma((steps, n)),
            dma((steps, n)),
        ],
        compiler_params=pltpu.CompilerParams(
            collective_id=0, has_side_effects=True, vmem_limit_bytes=48 * 1024 * 1024
        ),
        cost_estimate=pl.CostEstimate(
            flops=2 * trades * columns * (features + slots),
            bytes_accessed=4 * 1024 * 1024, transcendentals=0,
        ),
    )(coefficients, basis, trade_set[None, :], option_flag[None, :], lags)
    return out.reshape(SETS_DEV, dates, scenarios)


def solution(mesh):
    placed = (P("trade", None), P("trade", None, "scen"), P("trade"), P("trade"), P("trade"))
    return jax.shard_map(
        body, mesh=mesh, in_specs=placed, out_specs=P("trade", None, "scen"), check_vma=False
    )
```

```python
import functools

import jax
import jax.numpy as jnp
from jax import lax
from jax.experimental import pallas as pl
from jax.experimental.pallas import tpu as pltpu
from jax.sharding import PartitionSpec as P

SETS_DEV = 64
CAP = 8
LAG_MAX = 3
LANES = 128
INNER = 4
DATES_STEP = 4
ROWS_STEP = 2048
CUTS = 2


def kernel(n, gathers, dates, coef_hbm, basis_ref, set_ref, flag_ref, lag_ref, out_ref,
           coef_ref, coef_sem, whole, floor, member, sums, send, recv, notes_out, notes_in, pick,
           bs_sem, br_sem, ns_sem, nr_sem, ps_sem, pr_sem):
    me = lax.axis_index("trade")
    slots = n * CAP
    trades = coef_ref.shape[0]
    steps = dates // DATES_STEP
    width = DATES_STEP * LANES

    load = pltpu.make_async_copy(coef_hbm, coef_ref, coef_sem)
    load.start()

    def remote(src, dst, s_sem, r_sem, to):
        return pltpu.make_async_remote_copy(
            src_ref=src, dst_ref=dst, send_sem=s_sem, recv_sem=r_sem,
            device_id={"trade": to}, device_id_type=pl.DeviceIdType.MESH)

    def others(act):
        def go(k, carry):
            act(lax.rem(me + k, n))
            return carry
        lax.fori_loop(1, n, go, 0)

    barrier = pltpu.get_barrier_semaphore()
    others(lambda to: pl.semaphore_signal(
        barrier, inc=1, device_id={"trade": to}, device_id_type=pl.DeviceIdType.MESH))
    outer = n // INNER
    place, inner = me // INNER, lax.rem(me, INNER)
    core = lax.rem(inner, 2)
    sibling = place * INNER + inner - core + (1 - core)
    across = place * INNER + lax.rem(inner + 2, INNER)

    cut = dates * LANES // CUTS

    def block(part, owner, to, via):
        cols = pl.ds(part * cut, cut)
        src = basis_ref.at[:, cols] if owner is me else whole.at[owner, :, cols]
        return remote(src, whole.at[owner, :, cols], bs_sem.at[part, via, owner],
                      br_sem.at[part, owner], to)

    def pass_columns(part):
        for k in range(1, outer):
            owner = columns[k] * INNER + inner
            block(part, owner, owner, 0).wait_recv()
            block(part, owner, across, outer - 1).start()
            block(part, owner, sibling, outer).start()

    def pass_across(part):
        for k in range(outer):
            owner = columns[k] * INNER + lax.rem(inner + 2, INNER)
            block(part, owner, owner, 0).wait_recv()
            block(part, owner, sibling, outer).start()

    def end_gather(part):
        for pair in range(INNER // 2):
            for k in range(outer):
                owner = columns[k] * INNER + lax.rem(inner - core + (1 - core) + 2 * pair, INNER)
                block(part, owner, owner, 0).wait_recv()

    trade_set = set_ref[...]
    owner_row = trade_set // SETS_DEV
    local_row = trade_set - owner_row * SETS_DEV
    slot_of = lax.broadcasted_iota(jnp.int32, (slots, 1), 0)
    local_of = lax.broadcasted_iota(jnp.int32, (LANES, 1), 0)
    by_owner = (owner_row == slot_of // CAP).astype(jnp.float32).astype(jnp.bfloat16)
    by_local = (local_row == local_of).astype(jnp.float32).astype(jnp.bfloat16)
    counts = lax.dot_general(by_owner, by_local, (((1,), (1,)), ((), ())),
                             preferred_element_type=jnp.float32)
    present = counts > 0.5
    before = (lax.broadcasted_iota(jnp.int32, (LANES, LANES), 0)
              < lax.broadcasted_iota(jnp.int32, (LANES, LANES), 1))
    rank = jnp.dot(present.astype(jnp.float32).astype(jnp.bfloat16),
                   before.astype(jnp.float32).astype(jnp.bfloat16),
                   preferred_element_type=jnp.float32)
    chosen = present & (rank == lax.rem(slot_of, CAP).astype(jnp.float32))
    lane = lax.broadcasted_iota(jnp.int32, (slots, LANES), 1)
    local = jnp.sum(jnp.where(chosen, lane + 1, 0).astype(jnp.float32), axis=1, keepdims=True) - 1.0
    notes_out[:, 0:CAP] = jnp.broadcast_to(local, (slots, LANES)).reshape(n, CAP, LANES)
    notes_out[:, CAP:2 * CAP] = jnp.broadcast_to(lag_ref[...][None], (n, CAP, LANES))
    notes_in[me] = notes_out[me]
    name = jnp.where(local < 0.0, -1, local.astype(jnp.int32) + (slot_of // CAP) * SETS_DEV)
    member[...] = (name == trade_set).astype(jnp.float32).astype(jnp.bfloat16)

    if gathers:
        whole[me] = basis_ref[...]

    lowest = jnp.where(flag_ref[...] == 1, 0.0, -3.0e38).astype(jnp.float32)
    floor[...] = jnp.broadcast_to(lowest, (LANES, trades)).T

    sums[0:LAG_MAX] = jnp.zeros((LAG_MAX, slots, LANES), jnp.float32)

    pl.semaphore_wait(barrier, n - 1)
    columns = [lax.rem(place + k, outer) for k in range(outer)]
    if gathers:
        for part in range(CUTS):
            for k in range(1, outer):
                block(part, me, columns[k] * INNER + inner, k - 1).start()
            block(part, me, across, outer - 1).start()
            block(part, me, sibling, outer).start()

    def notes(to):
        return remote(notes_out.at[to], notes_in.at[me], ns_sem, nr_sem, to)

    others(lambda to: notes(to).start())
    if gathers:
        pass_columns(0)
        pass_across(0)
        for part in range(1, CUTS):
            pass_columns(part)

    all_notes = remote(notes_out.at[pl.ds(0, n - 1)], notes_in.at[pl.ds(0, n - 1)],
                       ns_sem, nr_sem, sibling)
    all_notes.wait_recv()
    known = notes_in[...]
    lag = jnp.sum(jnp.where(chosen, known[:, CAP:].reshape(slots, LANES), 0.0),
                  axis=1, keepdims=True)
    lag = jnp.broadcast_to(lag, (slots, LANES))
    ids = known[:, :CAP]
    ids = jnp.concatenate([ids, ids], axis=1).reshape(n * 2 * CAP, LANES)
    row = lax.broadcasted_iota(jnp.int32, (n * 2 * CAP, LANES), 0)
    lane = lax.broadcasted_iota(jnp.int32, (n * 2 * CAP, LANES), 1)
    same = (lax.rem(row, 2 * CAP) // CAP) == lane // SETS_DEV
    hit = same & (ids == lax.rem(lane, SETS_DEV).astype(jnp.float32))
    pick[...] = jnp.where(hit, 1.0, 0.0).astype(jnp.float32).T.astype(jnp.bfloat16)

    load.wait()
    if gathers:
        end_gather(0)

    def basis_at(c):
        cols = pl.ds(pl.multiple_of(c * width, width), width)
        if gathers:
            return whole[:, :, cols].reshape(-1, width)
        return basis_ref[:, cols]

    def piece(c, to):
        return remote(send.at[c, to], recv.at[c, me], ps_sem.at[c], pr_sem.at[c], to)

    def pieces(c):
        most = pl.ds(0, n - 1)
        return remote(send.at[c, most], recv.at[c, most], ps_sem.at[c], pr_sem.at[c], sibling)

    def step(c, carry):
        basis = basis_at(c)
        total = jnp.zeros((slots, width), jnp.float32)
        for first in range(0, trades, ROWS_STEP):
            rows = pl.ds(first, ROWS_STEP)
            valued = jnp.dot(coef_ref[rows, :], basis, preferred_element_type=jnp.float32)
            valued = jnp.maximum(valued, jnp.concatenate([floor[rows, :]] * DATES_STEP, axis=1))
            total += jnp.dot(member[:, rows], valued.astype(jnp.bfloat16),
                             preferred_element_type=jnp.float32)
        for d in range(DATES_STEP):
            sums[LAG_MAX + d] = total[:, d * LANES:(d + 1) * LANES]
        for half in range(DATES_STEP // 2):
            both = []
            for parity in range(2):
                at = LAG_MAX + 2 * half + parity
                collateral = jnp.zeros((slots, LANES), jnp.float32)
                for offset in range(1, LAG_MAX + 1):
                    collateral = jnp.where(lag == float(offset), sums[at - offset], collateral)
                both.append((sums[at] - collateral).reshape(n, CAP, LANES))
            send[c, :, half] = jnp.concatenate(both, axis=1).astype(jnp.bfloat16)
        for k in range(LAG_MAX):
            sums[k] = sums[DATES_STEP + k]
        recv[c, me] = send[c, me]
        others(lambda to: piece(c, to).start())
        return carry

    per_cut = steps // CUTS
    for part in range(CUTS):
        if gathers and part > 0:
            end_gather(part)
        lax.fori_loop(part * per_cut, part * per_cut + 1, step, 0)
        if gathers and part + 1 < CUTS:
            pass_across(part + 1)
        lax.fori_loop(part * per_cut + 1, (part + 1) * per_cut, step, 0)

    def finish(c, carry):
        pieces(c).wait_recv()
        for half in range(DATES_STEP // 2):
            result = jnp.dot(pick[...], recv[c, :, half].reshape(n * 2 * CAP, LANES),
                             preferred_element_type=jnp.float32)
            result = jnp.maximum(result, 0.0)
            for parity in range(2):
                at = pl.multiple_of((c * DATES_STEP + 2 * half + parity) * LANES, LANES)
                out_ref[:, pl.ds(at, LANES)] = result[parity * SETS_DEV:(parity + 1) * SETS_DEV]
        return carry

    lax.fori_loop(0, steps, finish, 0)

    if gathers:
        for part in range(CUTS):
            for k in range(1, outer):
                block(part, me, me, k - 1).wait_send()
            for k in range(outer):
                owner = columns[k] * INNER + inner
                block(part, owner, across, outer - 1).wait_send()
                block(part, owner, sibling, outer).wait_send()
                owner = columns[k] * INNER + lax.rem(inner + 2, INNER)
                block(part, owner, sibling, outer).wait_send()

    all_notes.wait_send()
    for c in range(steps):
        pieces(c).wait_send()


def body(coefficients, scenario_basis, trade_set, option_flag, margin_lag):
    n = lax.axis_size("trade")
    share, dates, scenarios = scenario_basis.shape
    trades, features = coefficients.shape
    columns = dates * scenarios
    gathers = share % 16 == 0 and n % INNER == 0
    basis = scenario_basis.reshape(share, columns)
    if not gathers:
        basis = lax.all_gather(basis, "trade", axis=0, tiled=True)
    lags = jnp.pad(margin_lag.astype(jnp.float32), (0, LANES - SETS_DEV))
    lags = jnp.broadcast_to(lags[None, :], (CAP, LANES))
    slots = n * CAP
    steps = dates // DATES_STEP
    halves = DATES_STEP // 2
    dma = pltpu.SemaphoreType.DMA
    whole = (n, share, columns) if gathers else (1, 16, LANES)
    out = pl.pallas_call(
        functools.partial(kernel, n, gathers, dates),
        out_shape=jax.ShapeDtypeStruct((SETS_DEV, columns), jnp.float32),
        in_specs=[pl.BlockSpec(memory_space=pl.ANY)] + [pl.BlockSpec(memory_space=pltpu.VMEM)] * 4,
        out_specs=pl.BlockSpec(memory_space=pltpu.VMEM),
        scratch_shapes=[
            pltpu.VMEM((trades, features), jnp.bfloat16),
            dma(()),
            pltpu.VMEM(whole, jnp.bfloat16),
            pltpu.VMEM((trades, LANES), jnp.float32),
            pltpu.VMEM((slots, trades), jnp.bfloat16),
            pltpu.VMEM((LAG_MAX + DATES_STEP, slots, LANES), jnp.float32),
            pltpu.VMEM((steps, n, halves, 2 * CAP, LANES), jnp.bfloat16),
            pltpu.VMEM((steps, n, halves, 2 * CAP, LANES), jnp.bfloat16),
            pltpu.VMEM((n, 2 * CAP, LANES), jnp.float32),
            pltpu.VMEM((n, 2 * CAP, LANES), jnp.float32),
            pltpu.VMEM((LANES, n * 2 * CAP), jnp.bfloat16),
            dma((CUTS, n // INNER + 1, n)),
            dma((CUTS, n)),
            dma(()),
            dma(()),
            dma((steps,)),
            dma((steps,)),
        ],
        compiler_params=pltpu.CompilerParams(
            collective_id=0, has_side_effects=True, vmem_limit_bytes=48 * 1024 * 1024
        ),
        cost_estimate=pl.CostEstimate(
            flops=2 * trades * columns * (features + slots),
            bytes_accessed=4 * 1024 * 1024, transcendentals=0,
        ),
    )(coefficients, basis, trade_set[None, :], option_flag[None, :], lags)
    return out.reshape(SETS_DEV, dates, scenarios)


def solution(mesh):
    placed = (P("trade", None), P("trade", None, "scen"), P("trade"), P("trade"), P("trade"))
    return jax.shard_map(
        body, mesh=mesh, in_specs=placed, out_specs=P("trade", None, "scen"), check_vma=False
    )
```

```python
import functools

import jax
import jax.numpy as jnp
from jax import lax
from jax.experimental import pallas as pl
from jax.experimental.pallas import tpu as pltpu
from jax.sharding import PartitionSpec as P

SETS_DEV = 64
CAP = 8
LAG_MAX = 3
LANES = 128
INNER = 4
DATES_STEP = 8
ROWS_STEP = 2048
CUTS = 2


def kernel(n, gathers, dates, coef_hbm, basis_ref, set_ref, flag_ref, lag_ref, out_ref,
           coef_ref, coef_sem, whole, floor, member, sums, send, recv, notes_out, notes_in, pick,
           bs_sem, br_sem, ns_sem, nr_sem, ps_sem, pr_sem):
    me = lax.axis_index("trade")
    slots = n * CAP
    trades = coef_ref.shape[0]
    steps = dates // DATES_STEP
    width = DATES_STEP * LANES

    load = pltpu.make_async_copy(coef_hbm, coef_ref, coef_sem)
    load.start()

    def remote(src, dst, s_sem, r_sem, to):
        return pltpu.make_async_remote_copy(
            src_ref=src, dst_ref=dst, send_sem=s_sem, recv_sem=r_sem,
            device_id={"trade": to}, device_id_type=pl.DeviceIdType.MESH)

    def others(act):
        def go(k, carry):
            act(lax.rem(me + k, n))
            return carry
        lax.fori_loop(1, n, go, 0)

    barrier = pltpu.get_barrier_semaphore()
    others(lambda to: pl.semaphore_signal(
        barrier, inc=1, device_id={"trade": to}, device_id_type=pl.DeviceIdType.MESH))
    outer = n // INNER
    place, inner = me // INNER, lax.rem(me, INNER)
    core = lax.rem(inner, 2)
    sibling = place * INNER + inner - core + (1 - core)
    across = place * INNER + lax.rem(inner + 2, INNER)

    cut = dates * LANES // CUTS

    def block(part, owner, to, via):
        cols = pl.ds(part * cut, cut)
        src = basis_ref.at[:, cols] if owner is me else whole.at[owner, :, cols]
        return remote(src, whole.at[owner, :, cols], bs_sem.at[part, via, owner],
                      br_sem.at[part, owner], to)

    def pass_columns(part):
        for k in range(1, outer):
            owner = columns[k] * INNER + inner
            block(part, owner, owner, 0).wait_recv()
            block(part, owner, across, outer - 1).start()
            block(part, owner, sibling, outer).start()

    def pass_across(part):
        for k in range(outer):
            owner = columns[k] * INNER + lax.rem(inner + 2, INNER)
            block(part, owner, owner, 0).wait_recv()
            block(part, owner, sibling, outer).start()

    def end_gather(part):
        for pair in range(INNER // 2):
            for k in range(outer):
                owner = columns[k] * INNER + lax.rem(inner - core + (1 - core) + 2 * pair, INNER)
                block(part, owner, owner, 0).wait_recv()

    trade_set = set_ref[...]
    owner_row = trade_set // SETS_DEV
    local_row = trade_set - owner_row * SETS_DEV
    slot_of = lax.broadcasted_iota(jnp.int32, (slots, 1), 0)
    local_of = lax.broadcasted_iota(jnp.int32, (LANES, 1), 0)
    by_owner = (owner_row == slot_of // CAP).astype(jnp.float32).astype(jnp.bfloat16)
    by_local = (local_row == local_of).astype(jnp.float32).astype(jnp.bfloat16)
    counts = lax.dot_general(by_owner, by_local, (((1,), (1,)), ((), ())),
                             preferred_element_type=jnp.float32)
    present = counts > 0.5
    before = (lax.broadcasted_iota(jnp.int32, (LANES, LANES), 0)
              < lax.broadcasted_iota(jnp.int32, (LANES, LANES), 1))
    rank = jnp.dot(present.astype(jnp.float32).astype(jnp.bfloat16),
                   before.astype(jnp.float32).astype(jnp.bfloat16),
                   preferred_element_type=jnp.float32)
    chosen = present & (rank == lax.rem(slot_of, CAP).astype(jnp.float32))
    lane = lax.broadcasted_iota(jnp.int32, (slots, LANES), 1)
    local = jnp.sum(jnp.where(chosen, lane + 1, 0).astype(jnp.float32), axis=1, keepdims=True) - 1.0
    notes_out[:, 0:CAP] = jnp.broadcast_to(local, (slots, LANES)).reshape(n, CAP, LANES)
    notes_out[:, CAP:2 * CAP] = jnp.broadcast_to(lag_ref[...][None], (n, CAP, LANES))
    notes_in[me] = notes_out[me]
    name = jnp.where(local < 0.0, -1, local.astype(jnp.int32) + (slot_of // CAP) * SETS_DEV)
    member[...] = (name == trade_set).astype(jnp.float32).astype(jnp.bfloat16)

    if gathers:
        whole[me] = basis_ref[...]

    lowest = jnp.where(flag_ref[...] == 1, 0.0, -3.0e38).astype(jnp.float32)
    floor[...] = jnp.broadcast_to(lowest, (LANES, trades)).T

    sums[0:LAG_MAX] = jnp.zeros((LAG_MAX, slots, LANES), jnp.float32)

    pl.semaphore_wait(barrier, n - 1)
    columns = [lax.rem(place + k, outer) for k in range(outer)]
    if gathers:
        for part in range(CUTS):
            for k in range(1, outer):
                block(part, me, columns[k] * INNER + inner, k - 1).start()
            block(part, me, across, outer - 1).start()
            block(part, me, sibling, outer).start()

    def notes(to):
        return remote(notes_out.at[to], notes_in.at[me], ns_sem, nr_sem, to)

    if gathers:
        pass_columns(0)
    others(lambda to: notes(to).start())
    if gathers:
        pass_across(0)
        for part in range(1, CUTS):
            pass_columns(part)

    all_notes = remote(notes_out.at[pl.ds(0, n - 1)], notes_in.at[pl.ds(0, n - 1)],
                       ns_sem, nr_sem, sibling)
    all_notes.wait_recv()
    known = notes_in[...]
    lag = jnp.sum(jnp.where(chosen, known[:, CAP:].reshape(slots, LANES), 0.0),
                  axis=1, keepdims=True)
    lag = jnp.broadcast_to(lag, (slots, LANES))
    ids = known[:, :CAP]
    ids = jnp.concatenate([ids, ids], axis=1).reshape(n * 2 * CAP, LANES)
    row = lax.broadcasted_iota(jnp.int32, (n * 2 * CAP, LANES), 0)
    lane = lax.broadcasted_iota(jnp.int32, (n * 2 * CAP, LANES), 1)
    same = (lax.rem(row, 2 * CAP) // CAP) == lane // SETS_DEV
    hit = same & (ids == lax.rem(lane, SETS_DEV).astype(jnp.float32))
    pick[...] = jnp.where(hit, 1.0, 0.0).astype(jnp.float32).T.astype(jnp.bfloat16)

    load.wait()
    if gathers:
        end_gather(0)

    def basis_at(c):
        cols = pl.ds(pl.multiple_of(c * width, width), width)
        if gathers:
            return whole[:, :, cols].reshape(-1, width)
        return basis_ref[:, cols]

    def piece(c, to):
        return remote(send.at[c, to], recv.at[c, me], ps_sem.at[c], pr_sem.at[c], to)

    def pieces(c):
        most = pl.ds(0, n - 1)
        return remote(send.at[c, most], recv.at[c, most], ps_sem.at[c], pr_sem.at[c], sibling)

    def step(c, carry):
        basis = basis_at(c)
        total = jnp.zeros((slots, width), jnp.float32)
        for first in range(0, trades, ROWS_STEP):
            rows = pl.ds(first, ROWS_STEP)
            valued = jnp.dot(coef_ref[rows, :], basis, preferred_element_type=jnp.float32)
            valued = jnp.maximum(valued, jnp.concatenate([floor[rows, :]] * DATES_STEP, axis=1))
            total += jnp.dot(member[:, rows], valued.astype(jnp.bfloat16),
                             preferred_element_type=jnp.float32)
        for d in range(DATES_STEP):
            sums[LAG_MAX + d] = total[:, d * LANES:(d + 1) * LANES]
        for half in range(DATES_STEP // 2):
            both = []
            for parity in range(2):
                at = LAG_MAX + 2 * half + parity
                collateral = jnp.zeros((slots, LANES), jnp.float32)
                for offset in range(1, LAG_MAX + 1):
                    collateral = jnp.where(lag == float(offset), sums[at - offset], collateral)
                both.append((sums[at] - collateral).reshape(n, CAP, LANES))
            send[c, :, half] = jnp.concatenate(both, axis=1).astype(jnp.bfloat16)
        for k in range(LAG_MAX):
            sums[k] = sums[DATES_STEP + k]
        recv[c, me] = send[c, me]
        others(lambda to: piece(c, to).start())
        return carry

    per_cut = steps // CUTS
    for part in range(CUTS):
        if gathers and part > 0:
            end_gather(part)
        lax.fori_loop(part * per_cut, part * per_cut + 1, step, 0)
        if gathers and part + 1 < CUTS:
            pass_across(part + 1)
        lax.fori_loop(part * per_cut + 1, (part + 1) * per_cut, step, 0)

    def finish(c, carry):
        pieces(c).wait_recv()
        for half in range(DATES_STEP // 2):
            result = jnp.dot(pick[...], recv[c, :, half].reshape(n * 2 * CAP, LANES),
                             preferred_element_type=jnp.float32)
            result = jnp.maximum(result, 0.0)
            for parity in range(2):
                at = pl.multiple_of((c * DATES_STEP + 2 * half + parity) * LANES, LANES)
                out_ref[:, pl.ds(at, LANES)] = result[parity * SETS_DEV:(parity + 1) * SETS_DEV]
        return carry

    lax.fori_loop(0, steps, finish, 0)

    if gathers:
        for part in range(CUTS):
            for k in range(1, outer):
                block(part, me, me, k - 1).wait_send()
            for k in range(outer):
                owner = columns[k] * INNER + inner
                block(part, owner, across, outer - 1).wait_send()
                block(part, owner, sibling, outer).wait_send()
                owner = columns[k] * INNER + lax.rem(inner + 2, INNER)
                block(part, owner, sibling, outer).wait_send()

    all_notes.wait_send()
    for c in range(steps):
        pieces(c).wait_send()


def body(coefficients, scenario_basis, trade_set, option_flag, margin_lag):
    n = lax.axis_size("trade")
    share, dates, scenarios = scenario_basis.shape
    trades, features = coefficients.shape
    columns = dates * scenarios
    gathers = share % 16 == 0 and n % INNER == 0
    basis = scenario_basis.reshape(share, columns)
    if not gathers:
        basis = lax.all_gather(basis, "trade", axis=0, tiled=True)
    lags = jnp.pad(margin_lag.astype(jnp.float32), (0, LANES - SETS_DEV))
    lags = jnp.broadcast_to(lags[None, :], (CAP, LANES))
    slots = n * CAP
    steps = dates // DATES_STEP
    halves = DATES_STEP // 2
    dma = pltpu.SemaphoreType.DMA
    whole = (n, share, columns) if gathers else (1, 16, LANES)
    out = pl.pallas_call(
        functools.partial(kernel, n, gathers, dates),
        out_shape=jax.ShapeDtypeStruct((SETS_DEV, columns), jnp.float32),
        in_specs=[pl.BlockSpec(memory_space=pl.ANY)] + [pl.BlockSpec(memory_space=pltpu.VMEM)] * 4,
        out_specs=pl.BlockSpec(memory_space=pltpu.VMEM),
        scratch_shapes=[
            pltpu.VMEM((trades, features), jnp.bfloat16),
            dma(()),
            pltpu.VMEM(whole, jnp.bfloat16),
            pltpu.VMEM((trades, LANES), jnp.float32),
            pltpu.VMEM((slots, trades), jnp.bfloat16),
            pltpu.VMEM((LAG_MAX + DATES_STEP, slots, LANES), jnp.float32),
            pltpu.VMEM((steps, n, halves, 2 * CAP, LANES), jnp.bfloat16),
            pltpu.VMEM((steps, n, halves, 2 * CAP, LANES), jnp.bfloat16),
            pltpu.VMEM((n, 2 * CAP, LANES), jnp.float32),
            pltpu.VMEM((n, 2 * CAP, LANES), jnp.float32),
            pltpu.VMEM((LANES, n * 2 * CAP), jnp.bfloat16),
            dma((CUTS, n // INNER + 1, n)),
            dma((CUTS, n)),
            dma(()),
            dma(()),
            dma((steps,)),
            dma((steps,)),
        ],
        compiler_params=pltpu.CompilerParams(
            collective_id=0, has_side_effects=True, vmem_limit_bytes=48 * 1024 * 1024
        ),
        cost_estimate=pl.CostEstimate(
            flops=2 * trades * columns * (features + slots),
            bytes_accessed=4 * 1024 * 1024, transcendentals=0,
        ),
    )(coefficients, basis, trade_set[None, :], option_flag[None, :], lags)
    return out.reshape(SETS_DEV, dates, scenarios)


def solution(mesh):
    placed = (P("trade", None), P("trade", None, "scen"), P("trade"), P("trade"), P("trade"))
    return jax.shard_map(
        body, mesh=mesh, in_specs=placed, out_specs=P("trade", None, "scen"), check_vma=False
    )
```
